32 devices in a mesh: gx: 4 (over y, x), gy: 2 (over core), gz: 4 (over z).
Axes of the slice: x: 2, y: 2, z: 4, core: 2. Of those that a mesh axis runs over, the one named last changes fastest.
Arguments:
- press_prev: float32 [64, 64, 512], P('gx', 'gy', 'gz'), may hold values from -6 to 6
- press_now: float32 [64, 64, 512], P('gx', 'gy', 'gz'), may hold values from -6 to 6
- board_prev: float32 [64, 64], P('gx', 'gy'), may hold values from -6 to 6
- board_now: float32 [64, 64], P('gx', 'gy'), may hold values from -6 to 6
- costate_prev: float32 [64, 64, 512], P('gx', 'gy', 'gz'), may hold values from -6 to 6
- costate_now: float32 [64, 64, 512], P('gx', 'gy', 'gz'), may hold values from -6 to 6
- adjoint_prev: float32 [64, 64], P('gx', 'gy'), may hold values from -6 to 6
- adjoint_now: float32 [64, 64], P('gx', 'gy'), may hold values from -6 to 6
- speed: float32 [64, 64, 512], P('gx', 'gy', 'gz'), may hold values from 0.12 to 0.32
- stiffness: float32 [64, 64], P('gx', 'gy'), may hold values from 0.4 to 1.6
- plate_mask: int32 [64, 64], P('gx', 'gy'), may hold values 0 or 1
- height: int32 [64, 64], P('gx', 'gy'), may hold values from 193 to 318
- source_cells: int32 [88], replicated, may hold values from 0 to 4095
- source_force: float32 [4, 88], replicated, may hold values from -12 to 12
Outputs:
- costate_first: float32 [64, 64, 512], P('gx', 'gy', 'gz')
- costate_second: float32 [64, 64, 512], P('gx', 'gy', 'gz')
- adjoint_first: float32 [64, 64], P('gx', 'gy')
- adjoint_second: float32 [64, 64], P('gx', 'gy')
- stiffness_grad: float32 [64, 64], P('gx', 'gy')
The draws below stay inside these ranges and needn't reach their ends.
Inputs may be any that keep to these rules, and one draw needn't show every extreme that they name: Every plate cell sits within 64 cells of the middle of the height. `source_cells`: flat indices of plate cells; points may repeat and may lie off the soundboard.
All inputs are finite; a program needn't handle non-finite values. No bound on the sum of `plate_mask` on one device may be relied on, other than what follows from the above.
Results may differ from the reference program's by a relative error of at most 0.022.
Values sent between devices are 32-bit elements; how exact they have to be, the bound alone decides.
A program may use at most 128 MiB of HBM per device.

```python
import math
import jax
import jax.numpy as jnp
from jax import lax

CZ = 128
STEPS = 4
NSRC = 88
NX = 64
NY = 64
NZ = 512


def set_ends(array, stream_key, least, top_value):
    spot = [jax.random.randint(jax.random.fold_in(stream_key, axis), (), 0, length) for axis, length in enumerate(array.shape)]
    widest = array.shape.index(max(array.shape))
    beside = spot[:widest] + [(spot[widest] + 1) % array.shape[widest]] + spot[widest + 1:]
    return array.at[tuple(spot)].set(least).at[tuple(beside)].set(top_value)


def block_levels(own_key, extent, cuts, low, high):
    gain = 1.0
    for axis_at, blocks in cuts:
        heights = jax.random.uniform(jax.random.fold_in(jax.random.fold_in(own_key, 6), axis_at), (blocks,), jnp.float32, low / len(cuts), high / len(cuts))
        gain = gain * jnp.repeat(jnp.exp(heights), extent[axis_at] // blocks).reshape((-1,) + (1,) * (len(extent) - 1 - axis_at))
    return gain


def normal_values(own_key, shape, scale, limit, split=(), held_as=jnp.bfloat16):
    array = jax.random.normal(own_key, shape, jnp.float32) * scale
    if len(split) > 0:
        array = block_levels(own_key, shape, split, -0.22, 0.18) * array
    return jnp.clip(array, min=-limit, max=limit).astype(held_as)


def setup_inputs(seed: int = 0) -> dict:
    seeds = jax.random.split(jax.random.key(seed), 15)
    return {
        "press_prev": normal_values(seeds[0], (NX, NY, NZ), 1.0, 6.0, ((0, 4), (1, 2), (2, 4)), jnp.float32),
        "press_now": normal_values(seeds[1], (NX, NY, NZ), 1.0, 6.0, ((0, 4), (1, 2), (2, 4)), jnp.float32),
        "board_prev": normal_values(seeds[2], (NX, NY), 1.0, 6.0, ((0, 4), (1, 2)), jnp.float32),
        "board_now": normal_values(seeds[3], (NX, NY), 1.0, 6.0, ((0, 4), (1, 2)), jnp.float32),
        "costate_prev": normal_values(seeds[4], (NX, NY, NZ), 1.0, 6.0, ((0, 4), (1, 2), (2, 4)), jnp.float32),
        "costate_now": normal_values(seeds[5], (NX, NY, NZ), 1.0, 6.0, ((0, 4), (1, 2), (2, 4)), jnp.float32),
        "adjoint_prev": normal_values(seeds[6], (NX, NY), 1.0, 6.0, ((0, 4), (1, 2)), jnp.float32),
        "adjoint_now": normal_values(seeds[7], (NX, NY), 1.0, 6.0, ((0, 4), (1, 2)), jnp.float32),
        "speed": jnp.clip(0.12 + 0.19999999552965164 * jax.random.uniform(seeds[8], (NX, NY, NZ), jnp.float32) ** block_levels(seeds[8], (NX, NY, NZ), ((0, 4), (1, 2), (2, 4)), -0.2, 0.2), 0.12, 0.32),
        "stiffness": jnp.clip(jnp.exp(math.log(1.6) - 1.3862944 * jax.random.uniform(seeds[9], (NX, NY), jnp.float32) ** block_levels(seeds[9], (NX, NY), ((0, 4), (1, 2)), -0.2, 0.2)), 0.4, 1.6),
        "plate_mask": set_ends((jax.random.randint(seeds[10], (NX, NY), 0, 4) < 3).astype(jnp.int32), jax.random.fold_in(seeds[10], 1), 0, 1),
        "height": set_ends(jax.random.randint(seeds[11], (NX, NY), NZ // 2 - CZ // 2 + 1, NZ // 2 + CZ // 2 - 1), jax.random.fold_in(seeds[11], 1), NZ // 2 - CZ // 2 + 1, (NZ // 2 + CZ // 2 - 1) - 1).astype(jnp.int32),
        "source_cells": set_ends(jax.random.randint(seeds[12], (NSRC,), 0, NX * NY), jax.random.fold_in(seeds[12], 1), 0, (NX * NY) - 1).astype(jnp.int32),
        "source_force": normal_values(seeds[13], (STEPS, NSRC), 2.0, 12.0, (), jnp.float32),
    }


DRIVE_GAIN = 0.5
LOAD_GAIN = 0.5
BEND_GAIN = 0.035

def lap_cube(field):
    padded = jnp.pad(field, 1)
    total = padded[2:, 1:-1, 1:-1] + padded[:-2, 1:-1, 1:-1]
    total = total + padded[1:-1, 2:, 1:-1] + padded[1:-1, :-2, 1:-1]
    total = total + padded[1:-1, 1:-1, 2:] + padded[1:-1, 1:-1, :-2]
    return total - 6.0 * field

def lap_sheet(field):
    padded = jnp.pad(field, 1)
    total = padded[2:, 1:-1] + padded[:-2, 1:-1] + padded[1:-1, 2:] + padded[1:-1, :-2]
    return total - 4.0 * field

def forward(press_old, press_cur, board_old, board_cur, stiffness, speed, dipole, mask_f, forcing):
    for counter in range(STEPS):
        press_next = 2.0 * press_cur - press_old + speed * lap_cube(press_cur) + DRIVE_GAIN * (board_cur - board_old)[:, :, None] * dipole
        load = -lax.optimization_barrier(jnp.sum(press_cur * dipole, axis=2))
        bent = lap_sheet(stiffness * lap_sheet(board_cur))
        board_next = mask_f * (2.0 * board_cur - board_old - BEND_GAIN * bent + LOAD_GAIN * load + forcing[counter])
        press_old, press_cur = (press_cur, press_next)
        board_old, board_cur = (board_cur, board_next)
    return (press_old, press_cur, board_old, board_cur)

def reference(press_prev, press_now, board_prev, board_now, costate_prev, costate_now, adjoint_prev, adjoint_now, speed, stiffness, plate_mask, height, source_cells, source_force):
    mask_f = plate_mask.astype(jnp.float32)
    level = jax.lax.broadcasted_iota(jnp.int32, (NX, NY, NZ), 2)
    dipole = (level == (height + 1)[:, :, None]).astype(jnp.float32) - (level == (height - 1)[:, :, None]).astype(jnp.float32)
    xpos = source_cells // NY
    ypos = source_cells % NY
    forcing = jnp.zeros((STEPS, NX, NY), jnp.float32).at[:, xpos, ypos].add(source_force)

    def mapping(press_old, press_cur, board_old, board_cur, stiff):
        return forward(press_old, press_cur, board_old, board_cur, stiff, speed, dipole, mask_f, forcing)
    primal, pullback = jax.vjp(mapping, press_prev, press_now, mask_f * board_prev, mask_f * board_now, stiffness)
    result = pullback((costate_prev, costate_now, adjoint_prev, adjoint_now))
    return (result[0], result[1], result[2], result[3], result[4])
```

```python
import functools

import jax
import jax.numpy as jnp
from jax import lax
from jax.experimental import pallas as pl
from jax.experimental.pallas import tpu as pltpu
from jax.sharding import PartitionSpec as P

STEPS = 4

DRIVE_GAIN = 0.5
LOAD_GAIN = 0.5
BEND_GAIN = 0.035

F32 = jnp.float32
MESH = pl.DeviceIdType.MESH

LEFT = 8
HALF = 64
PAD = 8

KEYS = ("xm", "xp", "ym", "yp", "mm", "pp", "mp", "pm", "zm", "zp", "far")
OPPOSITE = {
    "xm": "xp", "xp": "xm", "ym": "yp", "yp": "ym", "mm": "pp", "pp": "mm",
    "mp": "pm", "pm": "mp", "zm": "zp", "zp": "zm", "far": "far",
}
OFFSET = {
    "xm": (-1, 0, 0), "xp": (1, 0, 0), "ym": (0, -1, 0), "yp": (0, 1, 0),
    "mm": (-1, -1, 0), "pp": (1, 1, 0), "mp": (-1, 1, 0), "pm": (1, -1, 0),
    "zm": (0, 0, -1), "zp": (0, 0, 1),
}


def kernel(counts, *refs):
    (
        a_pprev, a_pnow, a_bprev, a_bnow, a_qprev, a_qnow, a_aprev, a_anow,
        a_speed, a_stiff, a_mask, a_height, a_cells, a_force,
        o_first, o_second, o_afirst, o_asecond, o_grad,
        pold, press, qold, q, speed, field, todo, todo_f, dip,
        bprev, bnow, aprev, anow, stiff, maski, heighti, cells, force,
        packs, uext, sext, wext, curve, out_t, first, af, asec, grad,
        xs, xr, ys, yr, dr, zs, zr, fr,
        in_sem, out_sem, send_sem, recv_sem,
    ) = refs
    nx, ny, nz = speed.shape
    top = PAD + ny
    count_x, count_y, count_z = counts
    rows_y = ny * count_y
    low, high = count_z // 2 - 1, count_z // 2
    gx, gy, gz = (lax.axis_index(a) for a in ("gx", "gy", "gz"))
    me = (gx, gy, gz)

    loads = []
    own = pl.ds(PAD, ny)
    for source, target in (
        (a_qnow, q.at[0]), (a_speed, speed), (a_anow, anow), (a_bnow, bnow), (a_mask, maski),
        (a_stiff, stiff), (a_height, heighti), (a_pnow, press.at[0, :, own, :]),
        (a_aprev, aprev), (a_bprev, bprev), (a_cells, cells), (a_force, force),
        (a_qprev, qold), (a_pprev, pold),
    ):
        copy = pltpu.make_async_copy(source, target, in_sem.at[len(loads)])
        copy.start()
        loads.append(copy)

    def partner(key):
        if key == "far":
            half = count_z // 2
            return (gx, gy, jnp.where(gz < half, gz + half, gz - half))
        return tuple(m + o for m, o in zip(me, OFFSET[key]))

    def exists(key):
        if key == "far":
            return gz >= 0
        good = None
        for m, o, n in zip(me, OFFSET[key], counts):
            if o:
                here = m >= 1 if o < 0 else m <= n - 2
                good = here if good is None else jnp.logical_and(good, here)
        return good

    is_mid = jnp.logical_or(gz == low, gz == high)

    for buffer in (xr, yr, dr, zr, fr, packs):
        buffer[...] = jnp.zeros_like(buffer)
    for buffer in (field, press):
        for row in (0, top):
            if len(buffer.shape) == 3:
                buffer[:, row : row + 8, :] = jnp.zeros((nx, 8, nz), F32)
            else:
                buffer[:, :, row : row + 8, :] = jnp.zeros((buffer.shape[0], nx, 8, nz), F32)

    barrier = pltpu.get_barrier_semaphore()
    for key in KEYS:
        @pl.when(exists(key))
        def _(key=key):
            pl.semaphore_signal(barrier, inc=1, device_id=partner(key), device_id_type=MESH)
    peers = 0
    for key in KEYS:
        peers = peers + exists(key).astype(jnp.int32)
    pl.semaphore_wait(barrier, peers)

    def message(step, key, to):
        index = KEYS.index(OPPOSITE[key])
        side = {"m": 0, "p": 1}
        if key[0] == "x":
            size = (4 * ny, 3 * ny, 2 * ny, 2 * ny)[step]
            source = xs.at[step, side[key[1]], pl.ds(0, size), :]
            target = xr.at[step, 1 - side[key[1]], pl.ds(0, size), :]
        elif key[0] == "y":
            begin = 0 if step < 2 else nx
            size = 2 * nx + 8 - begin + (8 if step == 0 else 0)
            source = ys.at[step, side[key[1]], pl.ds(begin, size), :]
            target = yr.at[step, 1 - side[key[1]], pl.ds(begin, size), :]
        elif key[0] == "z":
            source = zs.at[step, side[key[1]]]
            target = zr.at[step, 1 - side[key[1]]]
        elif key == "far":
            source = zs.at[step, 0, pl.ds(ny, ny), :]
            target = fr.at[step]
        else:
            size = 16 if step == 0 else 8
            source = ys.at[step, side[key[1]], pl.ds(2 * nx, size), :]
            target = dr.at[step, index - 4, pl.ds(0, size), :]
        return pltpu.make_async_remote_copy(
            src_ref=source, dst_ref=target,
            send_sem=send_sem.at[step, KEYS.index(key)], recv_sem=recv_sem.at[step, index],
            device_id=to, device_id_type=MESH,
        )

    def send(step):
        for key in KEYS:
            @pl.when(is_mid if key == "far" else exists(key))
            def _(key=key):
                message(step, key, partner(key)).start()

    def arrive(step, keys):
        for key in keys:
            @pl.when(jnp.logical_not(is_mid) if key == "far" else exists(key))
            def _(key=key):
                message(step, OPPOSITE[key], partner(key)).wait_recv()

    def sent(step):
        for key in KEYS:
            @pl.when(is_mid if key == "far" else exists(key))
            def _(key=key):
                message(step, key, partner(key)).wait_send()

    lane = lax.broadcasted_iota(jnp.int32, (ny, nz), 1)
    first_z, last_z = lane == 0, lane == nz - 1
    zero = jnp.zeros((ny, nz), F32)

    def column(values, at):
        return lax.slice_in_dim(values, at, at + 1, axis=1)

    for copy in loads[2:7] + loads[8:10]:
        copy.wait()
    a, b = LEFT, LEFT + HALF
    mid = LEFT + HALF // 2
    packs[0, a : a + nx, 0:ny] = anow[...]
    packs[0, b : b + nx, 0:ny] = bnow[...]
    packs[1, a : a + nx, 0:ny] = aprev[...]
    packs[1, b : b + nx, 0:ny] = -bprev[...]
    packs[2, a : a + nx, 0:ny] = stiff[...]
    packs[2, b : b + nx, 0:ny] = stiff[...]
    packs[3, a : a + nx, 0:ny] = maski[...].astype(F32)
    packs[3, b : b + nx, 0:ny] = maski[...].astype(F32)
    packs[3, mid : mid + nx, 0:ny] = heighti[...].astype(F32)
    turned = [jnp.transpose(packs[i])[0:ny, :] for i in range(4)]
    backward = lane < HALF
    level = turned[3]
    in_half = jnp.bitwise_and(lane, HALF - 1)
    inside = jnp.logical_and(in_half >= LEFT, in_half < LEFT + nx)
    mask = jnp.where(inside, level, 0.0)
    u = mask * turned[0]
    v = jnp.where(backward, turned[1], mask * turned[1])
    rigid = turned[2]

    depth = (lane + gz * nz).astype(F32)
    for x in range(nx):
        h = column(level, mid + x)
        dip[x] = jnp.where(depth == h + 1.0, 1.0, 0.0) - jnp.where(depth == h - 1.0, 1.0, 0.0)

    def stage_plate(step, u):
        for side in range(2):
            xs[step, side, ny : 2 * ny, :] = u
        ys[step, 0, 2 * nx : 2 * nx + 8, :] = u[0:8]
        ys[step, 1, 2 * nx : 2 * nx + 8, :] = u[ny - 8 : ny]

    def gather_plate(step, target, values, x_row, y_row, d_row):
        def merge(left, centre, right):
            index = lane[0 : centre.shape[0]]
            place = jnp.bitwise_and(index, HALF - 1)
            return jnp.where(
                place < LEFT,
                pltpu.roll(left, nz - nx, 1),
                jnp.where(place < LEFT + nx, centre, pltpu.roll(right, nx, 1)),
            )

        target[PAD : PAD + ny, :] = merge(
            xr[step, 0, x_row : x_row + ny, :], values, xr[step, 1, x_row : x_row + ny, :]
        )
        rows = slice(d_row, d_row + 8)
        slot = {key: KEYS.index(key) - 4 for key in ("mm", "pp", "mp", "pm")}
        target[0:PAD, :] = merge(
            dr[step, slot["mm"], rows, :], yr[step, 0, y_row : y_row + 8, :],
            dr[step, slot["pm"], rows, :],
        )
        target[top : top + 8, :] = merge(
            dr[step, slot["mp"], rows, :], yr[step, 1, y_row : y_row + 8, :],
            dr[step, slot["pp"], rows, :],
        )

    def take_air(step, x, value, packed, forward):
        react, near, far = packed
        where = (b if forward else a) + x
        gain = -LOAD_GAIN if forward else DRIVE_GAIN
        here = lane == where
        total = jnp.sum(value * dip[x], axis=1, keepdims=True) * gain
        react = jnp.where(here, total, react)
        if forward and step >= 2:
            return (react, near, far)
        if forward:
            sending = value
            x_rows, y_rows = slice(2 * ny, 3 * ny), 0
        else:
            sending = speed[x] * value
            field[x, PAD : PAD + ny, :] = sending
            x_rows, y_rows = slice(0, ny), nx
        if x == 0:
            xs[step, 0, x_rows, :] = sending
        if x == nx - 1:
            xs[step, 1, x_rows, :] = sending
        ys[step, 0, y_rows + x : y_rows + x + 1, :] = sending[0:1]
        ys[step, 1, y_rows + x : y_rows + x + 1, :] = sending[ny - 1 : ny]
        near = jnp.where(here, column(sending, 0), near)
        far = jnp.where(here, column(sending, nz - 1), far)
        return (react, near, far)

    def stage_z(step, packed):
        react, near, far = packed
        zs[step, 0, 0:ny, :] = near
        zs[step, 1, 0:ny, :] = far
        zs[step, 0, ny : 2 * ny, :] = react
        zs[step, 1, ny : 2 * ny, :] = react

    stage_plate(0, u)
    for side in range(2):
        xs[0, side, 3 * ny : 4 * ny, :] = rigid
    ys[0, 0, 2 * nx + 8 : 2 * nx + 16, :] = rigid[0:8]
    ys[0, 1, 2 * nx + 8 : 2 * nx + 16, :] = rigid[ny - 8 : ny]
    packed = (zero, zero, zero)
    for copy in loads[0:2] + loads[7:8]:
        copy.wait()
    for x in range(nx):
        packed = take_air(0, x, q[0, x], packed, False)
        packed = take_air(0, x, press[0, x, PAD : PAD + ny, :], packed, True)
    stage_z(0, packed)
    send(0)

    for copy in loads[10:12]:
        copy.wait()
    points = cells.shape[1]
    spot = jnp.broadcast_to(cells[...], (nz, points))
    column_x = gx * nx + lax.broadcasted_iota(jnp.int32, (nz, points), 0) - b
    begin = column_x * rows_y
    hit_x = (spot >= begin) & (spot < begin + rows_y)
    hit_x = hit_x & (column_x >= gx * nx) & (column_x < gx * nx + nx)
    spot_y = jnp.broadcast_to(cells[...], (ny, points))
    if rows_y & (rows_y - 1) == 0:
        spot_y = jnp.bitwise_and(spot_y, rows_y - 1)
    else:
        spot_y = lax.rem(spot_y, rows_y)
    hit_y = spot_y == gy * ny + lax.broadcasted_iota(jnp.int32, (ny, points), 0)
    hit_x = jnp.where(hit_x, 1.0, 0.0).astype(F32)
    forcing = [
        lax.dot_general(
            jnp.where(hit_y, jnp.broadcast_to(force[t : t + 1, :], (ny, points)), 0.0),
            hit_x, (((1,), (1,)), ((), ())),
            precision=lax.Precision.HIGHEST, preferred_element_type=F32,
        )
        for t in range(STEPS - 1)
    ]
    for copy in loads[12:14]:
        copy.wait()

    def inner(ref, x):
        centre = ref[x, PAD : PAD + ny, :]
        total = ref[x, PAD - 1 : PAD - 1 + ny, :] + ref[x, PAD + 1 : PAD + 1 + ny, :]
        if x > 0:
            total = total + ref[x - 1, PAD : PAD + ny, :]
        if x < nx - 1:
            total = total + ref[x + 1, PAD : PAD + ny, :]
        total = total + jnp.where(first_z, 0.0, pltpu.roll(centre, 1, 1))
        total = total + jnp.where(last_z, 0.0, pltpu.roll(centre, nz - 1, 1))
        return total - 6.0 * centre

    for step in range(STEPS):
        pull = LOAD_GAIN * u
        drive = DRIVE_GAIN * (u + v)
        for x in range(nx):
            now = q[step, x]
            old = qold[x] if step == 0 else -q[step - 1, x]
            todo[x] = old + 2.0 * now + inner(field, x) - column(pull, a + x) * dip[x]
            if step < 2:
                now = press[step, x, PAD : PAD + ny, :]
                old = pold[x] if step == 0 else press[step - 1, x, PAD : PAD + ny, :]
                todo_f[x] = (
                    2.0 * now - old + speed[x] * inner(press.at[step], x)
                    + column(drive, b + x) * dip[x]
                )
        if step == STEPS - 1:
            for x in range(nx):
                first[x] = -q[step, x]
            copy_first = pltpu.make_async_copy(first, o_first, out_sem.at[0])
            copy_first.start()
        arrive(step, KEYS)

        gather_plate(step, uext, u, ny, 2 * nx, 0)
        if step == 0:
            gather_plate(step, sext, rigid, 3 * ny, 2 * nx + 8, 8)
        wide = slice(PAD - 4, PAD + ny + 4)
        centre = uext[wide, :]
        bend = (
            uext[PAD - 5 : PAD + ny + 3, :] + uext[PAD - 3 : PAD + ny + 5, :]
            + pltpu.roll(centre, 1, 1) + pltpu.roll(centre, nz - 1, 1) - 4.0 * centre
        )
        curve[step, wide, :] = bend
        wext[wide, :] = sext[wide, :] * bend
        centre = wext[PAD : PAD + ny, :]
        bent = (
            wext[PAD - 1 : PAD - 1 + ny, :] + wext[PAD + 1 : PAD + 1 + ny, :]
            + pltpu.roll(centre, 1, 1) + pltpu.roll(centre, nz - 1, 1) - 4.0 * centre
        )
        mine = packed[0]
        react = jnp.where(is_mid, mine, fr[step]) + jnp.where(
            gz <= low, zr[step, 1, ny : 2 * ny, :], zr[step, 0, ny : 2 * ny, :]
        )
        fresh = 2.0 * u + v - BEND_GAIN * bent + react
        if step < STEPS - 1:
            fresh = fresh + forcing[step]
        v = -u - jnp.where(backward, react, 0.0)
        u = mask * fresh
        if step < STEPS - 1:
            stage_plate(step + 1, u)

        packed = (zero, zero, zero)
        for x in range(nx):
            for row, side in ((0, 0), (ny - 1, 1)):
                todo[x, row : row + 1, :] = (
                    todo[x, row : row + 1, :] + yr[step, side, nx + x : nx + x + 1, :]
                )
                if step < 2:
                    todo_f[x, row : row + 1, :] = (
                        todo_f[x, row : row + 1, :]
                        + speed[x, row : row + 1, :] * yr[step, side, x : x + 1, :]
                    )
        below, above = zr[step, 0, 0:ny, :], zr[step, 1, 0:ny, :]

        def outer(x, base, x_rows):
            layer = jnp.where(first_z, column(below, base + x), 0.0)
            layer = jnp.where(last_z, column(above, base + x), layer)
            if x == 0:
                layer = layer + xr[step, 0, x_rows, :]
            if x == nx - 1:
                layer = layer + xr[step, 1, x_rows, :]
            return layer

        for x in range(nx):
            new = todo[x] + outer(x, a, slice(0, ny))
            q[step + 1, x] = new
            if step < STEPS - 1:
                packed = take_air(step + 1, x, new, packed, False)
            if step < 2:
                new = todo_f[x] + speed[x] * outer(x, b, slice(2 * ny, 3 * ny))
                if step == 0:
                    press[1, x, PAD : PAD + ny, :] = new
                packed = take_air(step + 1, x, new, packed, True)
        if step < STEPS - 1:
            stage_z(step + 1, packed)
            send(step + 1)

    copy_second = pltpu.make_async_copy(q.at[STEPS], o_second, out_sem.at[1])
    copy_second.start()
    slope = zero
    for step in range(STEPS):
        slope = slope + curve[STEPS - 1 - step, PAD : PAD + ny, :] * pltpu.roll(
            curve[step, PAD : PAD + ny, :], nz - HALF, 1
        )
    slope = -BEND_GAIN * slope
    third = nz // 4
    out = jnp.where(lane < third, v, jnp.where(lane < 2 * third, pltpu.roll(fresh, third, 1), pltpu.roll(slope, 2 * third, 1)))
    out_t[...] = jnp.zeros_like(out_t)
    out_t[0:ny, :] = out
    done = jnp.transpose(out_t[...])
    af[...] = done[LEFT : LEFT + nx, 0:ny]
    asec[...] = done[LEFT + third : LEFT + third + nx, 0:ny]
    grad[...] = done[LEFT + 2 * third : LEFT + 2 * third + nx, 0:ny]
    stores = [copy_first, copy_second]
    for source, target in ((af, o_afirst), (asec, o_asecond), (grad, o_grad)):
        copy = pltpu.make_async_copy(source, target, out_sem.at[len(stores)])
        copy.start()
        stores.append(copy)
    for step in range(STEPS):
        sent(step)
    for copy in stores:
        copy.wait()


def on_device(counts, press_prev, press_now, board_prev, board_now, costate_prev, costate_now,
              adjoint_prev, adjoint_now, speed, stiffness, plate_mask, height, source_cells,
              source_force):
    nx, ny, nz = speed.shape
    assert counts[2] == 4 and nz == 128 and nx == 16 and ny % 8 == 0
    points = source_cells.shape[0]
    air = jax.ShapeDtypeStruct((nx, ny, nz), F32)
    plate = jax.ShapeDtypeStruct((nx, ny), F32)
    tall = ny + 2 * PAD
    vmem = pltpu.VMEM
    sheet = vmem((nx, ny), F32)
    block = vmem((nx, ny, nz), F32)
    scratch = [
        block, vmem((2, nx, tall, nz), F32), block, vmem((STEPS + 1, nx, ny, nz), F32), block,
        vmem((nx, tall, nz), F32), block, block, block,
        sheet, sheet, sheet, sheet, sheet, vmem((nx, ny), jnp.int32), vmem((nx, ny), jnp.int32),
        vmem((1, points), jnp.int32), vmem(source_force.shape, F32),
        vmem((4, nz, nz), F32), vmem((tall, nz), F32), vmem((tall, nz), F32),
        vmem((tall, nz), F32), vmem((STEPS, tall, nz), F32), vmem((nz, nz), F32),
        block, sheet, sheet, sheet,
        vmem((STEPS, 2, 4 * ny, nz), F32), vmem((STEPS, 2, 4 * ny, nz), F32),
        vmem((STEPS, 2, 2 * nx + 16, nz), F32), vmem((STEPS, 2, 2 * nx + 16, nz), F32),
        vmem((STEPS, 4, 16, nz), F32),
        vmem((STEPS, 2, 2 * ny, nz), F32), vmem((STEPS, 2, 2 * ny, nz), F32),
        vmem((STEPS, ny, nz), F32),
        pltpu.SemaphoreType.DMA((14,)), pltpu.SemaphoreType.DMA((5,)),
        pltpu.SemaphoreType.DMA((STEPS, len(KEYS))), pltpu.SemaphoreType.DMA((STEPS, len(KEYS))),
    ]
    anywhere = pl.BlockSpec(memory_space=pl.ANY)
    return pl.pallas_call(
        functools.partial(kernel, counts),
        out_shape=(air, air, plate, plate, plate),
        in_specs=[anywhere] * 14,
        out_specs=(anywhere,) * 5,
        scratch_shapes=scratch,
        compiler_params=pltpu.CompilerParams(
            collective_id=0, has_side_effects=True, vmem_limit_bytes=40 * 1024 * 1024
        ),
        cost_estimate=pl.CostEstimate(
            flops=40 * 6 * nx * ny * nz, bytes_accessed=28 * nx * ny * nz, transcendentals=0
        ),
    )(
        press_prev, press_now, board_prev, board_now, costate_prev, costate_now, adjoint_prev,
        adjoint_now, speed, stiffness, plate_mask, height, source_cells.reshape(1, points),
        source_force,
    )


def solution(mesh):
    air, plate = P("gx", "gy", "gz"), P("gx", "gy")
    counts = tuple(mesh.shape[a] for a in ("gx", "gy", "gz"))
    return jax.shard_map(
        functools.partial(on_device, counts),
        mesh=mesh,
        in_specs=(air, air, plate, plate, air, air, plate, plate, air, plate, plate, plate, P(), P()),
        out_specs=(air, air, plate, plate, plate),
        check_vma=False,
    )
```

```python
import functools

import jax
import jax.numpy as jnp
from jax import lax
from jax.experimental import pallas as pl
from jax.experimental.pallas import tpu as pltpu
from jax.sharding import PartitionSpec as P

STEPS = 4

DRIVE_GAIN = 0.5
LOAD_GAIN = 0.5
BEND_GAIN = 0.035

F32 = jnp.float32
MESH = pl.DeviceIdType.MESH

LEFT = 8
HALF = 64
PAD = 8

KEYS = ("xm", "xp", "ym", "yp", "mm", "pp", "mp", "pm", "zm", "zp", "far")
OPPOSITE = {
    "xm": "xp", "xp": "xm", "ym": "yp", "yp": "ym", "mm": "pp", "pp": "mm",
    "mp": "pm", "pm": "mp", "zm": "zp", "zp": "zm", "far": "far",
}
OFFSET = {
    "xm": (-1, 0, 0), "xp": (1, 0, 0), "ym": (0, -1, 0), "yp": (0, 1, 0),
    "mm": (-1, -1, 0), "pp": (1, 1, 0), "mp": (-1, 1, 0), "pm": (1, -1, 0),
    "zm": (0, 0, -1), "zp": (0, 0, 1),
}


def kernel(counts, *refs):
    (
        a_pprev, a_pnow, a_bprev, a_bnow, a_qprev, a_qnow, a_aprev, a_anow,
        a_speed, a_stiff, a_mask, a_height, a_cells, a_force,
        o_first, o_second, o_afirst, o_asecond, o_grad,
        pold, press, qold, q, speed, field, todo, todo_f, dip,
        bprev, bnow, aprev, anow, stiff, maski, heighti, cells, force,
        packs, uext, sext, wext, curve, out_t,
        xs, xr, ys, yr, dr, zs, zr, fr,
        in_sem, send_sem, recv_sem,
    ) = refs
    nx, ny, nz = speed.shape
    top = PAD + ny
    count_x, count_y, count_z = counts
    rows_y = ny * count_y
    low, high = count_z // 2 - 1, count_z // 2
    gx, gy, gz = (lax.axis_index(a) for a in ("gx", "gy", "gz"))
    me = (gx, gy, gz)

    loads = []
    own = pl.ds(PAD, ny)
    for source, target in (
        (a_qnow, q.at[0]), (a_speed, speed), (a_anow, anow), (a_bnow, bnow), (a_mask, maski),
        (a_stiff, stiff), (a_height, heighti), (a_pnow, press.at[0, :, own, :]),
        (a_aprev, aprev), (a_bprev, bprev), (a_cells, cells), (a_force, force),
        (a_qprev, qold), (a_pprev, pold),
    ):
        copy = pltpu.make_async_copy(source, target, in_sem.at[len(loads)])
        copy.start()
        loads.append(copy)

    def partner(key):
        if key == "far":
            half = count_z // 2
            return (gx, gy, jnp.where(gz < half, gz + half, gz - half))
        return tuple(m + o for m, o in zip(me, OFFSET[key]))

    def exists(key):
        if key == "far":
            return gz >= 0
        good = None
        for m, o, n in zip(me, OFFSET[key], counts):
            if o:
                here = m >= 1 if o < 0 else m <= n - 2
                good = here if good is None else jnp.logical_and(good, here)
        return good

    is_mid = jnp.logical_or(gz == low, gz == high)

    for buffer in (xr, yr, dr, zr, fr, packs):
        buffer[...] = jnp.zeros_like(buffer)
    for buffer in (field, press):
        for row in (0, top):
            if len(buffer.shape) == 3:
                buffer[:, row : row + 8, :] = jnp.zeros((nx, 8, nz), F32)
            else:
                buffer[:, :, row : row + 8, :] = jnp.zeros((buffer.shape[0], nx, 8, nz), F32)

    barrier = pltpu.get_barrier_semaphore()
    for key in KEYS:
        @pl.when(exists(key))
        def _(key=key):
            pl.semaphore_signal(barrier, inc=1, device_id=partner(key), device_id_type=MESH)

    def message(step, key, to):
        index = KEYS.index(OPPOSITE[key])
        side = {"m": 0, "p": 1}
        if key[0] == "x":
            begin = 0 if step < 2 else ny
            size = 2 * ny + 8 - begin + (8 if step == 0 else 0)
            source = xs.at[step, side[key[1]], pl.ds(begin, size), :]
            target = xr.at[step, 1 - side[key[1]], pl.ds(begin, size), :]
        elif key[0] == "y":
            begin = 0 if step < 2 else nx
            size = 2 * nx + 8 - begin + (8 if step == 0 else 0)
            source = ys.at[step, side[key[1]], pl.ds(begin, size), :]
            target = yr.at[step, 1 - side[key[1]], pl.ds(begin, size), :]
        elif key[0] == "z":
            source = zs.at[step, side[key[1]]]
            target = zr.at[step, 1 - side[key[1]]]
        elif key == "far":
            source = zs.at[step, 0]
            target = fr.at[step]
        else:
            size = 16 if step == 0 else 8
            source = ys.at[step, side[key[1]], pl.ds(2 * nx, size), :]
            target = dr.at[step, index - 4, pl.ds(0, size), :]
        return pltpu.make_async_remote_copy(
            src_ref=source, dst_ref=target,
            send_sem=send_sem.at[step, KEYS.index(key)], recv_sem=recv_sem.at[step, index],
            device_id=to, device_id_type=MESH,
        )

    def send(step, keys):
        for key in keys:
            @pl.when(is_mid if key == "far" else exists(key))
            def _(key=key):
                message(step, key, partner(key)).start()

    def arrive(step, keys):
        for key in keys:
            @pl.when(jnp.logical_not(is_mid) if key == "far" else exists(key))
            def _(key=key):
                message(step, OPPOSITE[key], partner(key)).wait_recv()

    def sent(step):
        for key in KEYS:
            @pl.when(is_mid if key == "far" else exists(key))
            def _(key=key):
                message(step, key, partner(key)).wait_send()

    lane = lax.broadcasted_iota(jnp.int32, (ny, nz), 1)
    first_z, last_z = lane == 0, lane == nz - 1
    zero = jnp.zeros((ny, nz), F32)

    def column(values, at):
        return lax.slice_in_dim(values, at, at + 1, axis=1)

    for copy in loads[2:7] + loads[8:10]:
        copy.wait()
    a, b = LEFT, LEFT + HALF
    mid = LEFT + HALF // 2
    packs[0, a : a + nx, 0:ny] = anow[...]
    packs[0, b : b + nx, 0:ny] = bnow[...]
    packs[1, a : a + nx, 0:ny] = aprev[...]
    packs[1, b : b + nx, 0:ny] = -bprev[...]
    packs[2, a : a + nx, 0:ny] = stiff[...]
    packs[2, b : b + nx, 0:ny] = stiff[...]
    packs[3, a : a + nx, 0:ny] = maski[...].astype(F32)
    packs[3, b : b + nx, 0:ny] = maski[...].astype(F32)
    packs[3, mid : mid + nx, 0:ny] = heighti[...].astype(F32)
    turned = [jnp.transpose(packs[i])[0:ny, :] for i in range(4)]
    backward = lane < HALF
    level = turned[3]
    in_half = jnp.bitwise_and(lane, HALF - 1)
    inside = jnp.logical_and(in_half >= LEFT, in_half < LEFT + nx)
    mask = jnp.where(inside, level, 0.0)
    u = mask * turned[0]
    v = jnp.where(backward, turned[1], mask * turned[1])
    rigid = turned[2]

    depth = (lane + gz * nz).astype(F32)
    for x in range(nx):
        h = column(level, mid + x)
        dip[x] = jnp.where(depth == h + 1.0, 1.0, 0.0) - jnp.where(depth == h - 1.0, 1.0, 0.0)

    def shifted(values, by):
        by = by % nz
        return pltpu.roll(values, by, 1) if by else values

    chunk = jnp.bitwise_and(lane[0:8], HALF - 1) // 8

    def edge(values, side):
        begin = LEFT if side == 0 else LEFT + nx - 8
        out = zero[0:8]
        for c in range(ny // 8):
            out = jnp.where(chunk == c, shifted(values[8 * c : 8 * c + 8], 8 * c - begin), out)
        return out

    def unfold_edge(values, begin):
        return jnp.concatenate([shifted(values, begin - 8 * c) for c in range(ny // 8)], axis=0)

    def unfold_z(values):
        return jnp.concatenate([values, shifted(values, -nx)], axis=0)

    def stage_plate(step, u):
        for side in range(2):
            xs[step, side, 2 * ny : 2 * ny + 8, :] = edge(u, side)
        ys[step, 0, 2 * nx : 2 * nx + 8, :] = u[0:8]
        ys[step, 1, 2 * nx : 2 * nx + 8, :] = u[ny - 8 : ny]

    def gather_plate(step, target, values, x_row, y_row, d_row):
        def merge(left, centre, right):
            index = lane[0 : centre.shape[0]]
            place = jnp.bitwise_and(index, HALF - 1)
            return jnp.where(
                place < LEFT,
                left,
                jnp.where(place < LEFT + nx, centre, right),
            )

        target[PAD : PAD + ny, :] = merge(
            unfold_edge(xr[step, 0, x_row : x_row + 8, :], LEFT - 8), values,
            unfold_edge(xr[step, 1, x_row : x_row + 8, :], LEFT + nx),
        )
        rows = slice(d_row, d_row + 8)
        slot = {key: KEYS.index(key) - 4 for key in ("mm", "pp", "mp", "pm")}
        target[0:PAD, :] = merge(
            shifted(dr[step, slot["mm"], rows, :], -nx), yr[step, 0, y_row : y_row + 8, :],
            shifted(dr[step, slot["pm"], rows, :], nx),
        )
        target[top : top + 8, :] = merge(
            shifted(dr[step, slot["mp"], rows, :], -nx), yr[step, 1, y_row : y_row + 8, :],
            shifted(dr[step, slot["pp"], rows, :], nx),
        )

    def take_air(step, x, value, packed, forward):
        react, near, far = packed
        where = (b if forward else a) + x
        gain = -LOAD_GAIN if forward else DRIVE_GAIN
        here = lane == where
        total = jnp.sum(value * dip[x], axis=1, keepdims=True) * gain
        react = jnp.where(here, total, react)
        if forward and step >= 2:
            return (react, near, far)
        if forward:
            sending = value
            x_rows, y_rows = slice(0, ny), 0
        else:
            sending = speed[x] * value
            field[x, PAD : PAD + ny, :] = sending
            x_rows, y_rows = slice(ny, 2 * ny), nx
        if x == 0:
            xs[step, 0, x_rows, :] = sending
        if x == nx - 1:
            xs[step, 1, x_rows, :] = sending
        ys[step, 0, y_rows + x : y_rows + x + 1, :] = sending[0:1]
        ys[step, 1, y_rows + x : y_rows + x + 1, :] = sending[ny - 1 : ny]
        near = jnp.where(here, column(sending, 0), near)
        far = jnp.where(here, column(sending, nz - 1), far)
        return (react, near, far)

    def stage_z(step, packed):
        react, near, far = packed
        react = shifted(react, 2 * nx)
        for side, face in ((0, near), (1, far)):
            both = face + react
            zs[step, side] = both[0 : ny // 2] + shifted(both[ny // 2 : ny], nx)

    stage_plate(0, u)
    for side in range(2):
        xs[0, side, 2 * ny + 8 : 2 * ny + 16, :] = edge(rigid, side)
    ys[0, 0, 2 * nx + 8 : 2 * nx + 16, :] = rigid[0:8]
    ys[0, 1, 2 * nx + 8 : 2 * nx + 16, :] = rigid[ny - 8 : ny]
    packed = (zero, zero, zero)
    for copy in loads[0:2] + loads[7:8]:
        copy.wait()
    peers = 0
    for key in KEYS:
        peers = peers + exists(key).astype(jnp.int32)
    pl.semaphore_wait(barrier, peers)
    send(0, KEYS[4:8])
    order = (0, nx - 1) + tuple(range(1, nx - 1))
    for i, x in enumerate(order):
        packed = take_air(0, x, q[0, x], packed, False)
        packed = take_air(0, x, press[0, x, PAD : PAD + ny, :], packed, True)
        if i == 1:
            send(0, KEYS[0:2])
    stage_z(0, packed)
    send(0, KEYS[8:11] + KEYS[2:4])

    for copy in loads[10:12]:
        copy.wait()
    points = cells.shape[1]
    spot = jnp.broadcast_to(cells[...], (nz, points))
    column_x = gx * nx + lax.broadcasted_iota(jnp.int32, (nz, points), 0) - b
    begin = column_x * rows_y
    hit_x = (spot >= begin) & (spot < begin + rows_y)
    hit_x = hit_x & (column_x >= gx * nx) & (column_x < gx * nx + nx)
    spot_y = jnp.broadcast_to(cells[...], (ny, points))
    if rows_y & (rows_y - 1) == 0:
        spot_y = jnp.bitwise_and(spot_y, rows_y - 1)
    else:
        spot_y = lax.rem(spot_y, rows_y)
    hit_y = spot_y == gy * ny + lax.broadcasted_iota(jnp.int32, (ny, points), 0)
    hit_x = jnp.where(hit_x, 1.0, 0.0).astype(F32)
    forcing = [
        lax.dot_general(
            jnp.where(hit_y, jnp.broadcast_to(force[t : t + 1, :], (ny, points)), 0.0),
            hit_x, (((1,), (1,)), ((), ())),
            precision=lax.Precision.HIGHEST, preferred_element_type=F32,
        )
        for t in range(STEPS - 1)
    ]
    for copy in loads[12:14]:
        copy.wait()

    def inner(ref, x):
        centre = ref[x, PAD : PAD + ny, :]
        total = ref[x, PAD - 1 : PAD - 1 + ny, :] + ref[x, PAD + 1 : PAD + 1 + ny, :]
        if x > 0:
            total = total + ref[x - 1, PAD : PAD + ny, :]
        if x < nx - 1:
            total = total + ref[x + 1, PAD : PAD + ny, :]
        total = total + jnp.where(first_z, 0.0, pltpu.roll(centre, 1, 1))
        total = total + jnp.where(last_z, 0.0, pltpu.roll(centre, nz - 1, 1))
        return total - 6.0 * centre

    for step in range(STEPS):
        pull = LOAD_GAIN * u
        drive = DRIVE_GAIN * (u + v)
        for x in range(nx):
            now = q[step, x]
            old = qold[x] if step == 0 else -q[step - 1, x]
            todo[x] = old + 2.0 * now + inner(field, x) - column(pull, a + x) * dip[x]
            if step < 2:
                now = press[step, x, PAD : PAD + ny, :]
                old = pold[x] if step == 0 else press[step - 1, x, PAD : PAD + ny, :]
                todo_f[x] = (
                    2.0 * now - old + speed[x] * inner(press.at[step], x)
                    + column(drive, b + x) * dip[x]
                )
        if step == STEPS - 1:
            for x in range(nx):
                o_first[x] = -q[step, x]
        arrive(step, KEYS)

        gather_plate(step, uext, u, 2 * ny, 2 * nx, 0)
        if step == 0:
            gather_plate(step, sext, rigid, 2 * ny + 8, 2 * nx + 8, 8)
        wide = slice(PAD - 4, PAD + ny + 4)
        centre = uext[wide, :]
        bend = (
            uext[PAD - 5 : PAD + ny + 3, :] + uext[PAD - 3 : PAD + ny + 5, :]
            + pltpu.roll(centre, 1, 1) + pltpu.roll(centre, nz - 1, 1) - 4.0 * centre
        )
        curve[step, wide, :] = bend
        wext[wide, :] = sext[wide, :] * bend
        centre = wext[PAD : PAD + ny, :]
        bent = (
            wext[PAD - 1 : PAD - 1 + ny, :] + wext[PAD + 1 : PAD + 1 + ny, :]
            + pltpu.roll(centre, 1, 1) + pltpu.roll(centre, nz - 1, 1) - 4.0 * centre
        )
        mine = packed[0]
        below, above = unfold_z(zr[step, 0]), unfold_z(zr[step, 1])
        react = jnp.where(is_mid, mine, shifted(unfold_z(fr[step]), -2 * nx)) + shifted(
            jnp.where(gz <= low, above, below), -2 * nx
        )
        fresh = 2.0 * u + v - BEND_GAIN * bent + react
        if step < STEPS - 1:
            fresh = fresh + forcing[step]
        v = -u - jnp.where(backward, react, 0.0)
        u = mask * fresh
        if step < STEPS - 1:
            stage_plate(step + 1, u)
            send(step + 1, KEYS[4:8])

        packed = (zero, zero, zero)
        for x in range(nx):
            for row, side in ((0, 0), (ny - 1, 1)):
                todo[x, row : row + 1, :] = (
                    todo[x, row : row + 1, :] + yr[step, side, nx + x : nx + x + 1, :]
                )
                if step < 2:
                    todo_f[x, row : row + 1, :] = (
                        todo_f[x, row : row + 1, :]
                        + speed[x, row : row + 1, :] * yr[step, side, x : x + 1, :]
                    )
        def outer(x, base, x_rows):
            layer = jnp.where(first_z, column(below, base + x), 0.0)
            layer = jnp.where(last_z, column(above, base + x), layer)
            if x == 0:
                layer = layer + xr[step, 0, x_rows, :]
            if x == nx - 1:
                layer = layer + xr[step, 1, x_rows, :]
            return layer

        for i, x in enumerate(order):
            new = todo[x] + outer(x, a, slice(ny, 2 * ny))
            if step == STEPS - 1:
                o_second[x] = new
            else:
                q[step + 1, x] = new
                packed = take_air(step + 1, x, new, packed, False)
            if step < 2:
                new = todo_f[x] + speed[x] * outer(x, b, slice(0, ny))
                if step == 0:
                    press[1, x, PAD : PAD + ny, :] = new
                packed = take_air(step + 1, x, new, packed, True)
            if i == 1 and step < STEPS - 1:
                send(step + 1, KEYS[0:2])
        if step < STEPS - 1:
            stage_z(step + 1, packed)
            send(step + 1, KEYS[8:11] + KEYS[2:4])

    slope = zero
    for step in range(STEPS):
        slope = slope + curve[STEPS - 1 - step, PAD : PAD + ny, :] * pltpu.roll(
            curve[step, PAD : PAD + ny, :], nz - HALF, 1
        )
    slope = -BEND_GAIN * slope
    third = nz // 4
    out = jnp.where(lane < third, v, jnp.where(lane < 2 * third, pltpu.roll(fresh, third, 1), pltpu.roll(slope, 2 * third, 1)))
    out_t[...] = jnp.zeros_like(out_t)
    out_t[0:ny, :] = out
    done = jnp.transpose(out_t[...])
    o_afirst[...] = done[LEFT : LEFT + nx, 0:ny]
    o_asecond[...] = done[LEFT + third : LEFT + third + nx, 0:ny]
    o_grad[...] = done[LEFT + 2 * third : LEFT + 2 * third + nx, 0:ny]
    for step in range(STEPS):
        sent(step)


def on_device(counts, press_prev, press_now, board_prev, board_now, costate_prev, costate_now,
              adjoint_prev, adjoint_now, speed, stiffness, plate_mask, height, source_cells,
              source_force):
    nx, ny, nz = speed.shape
    assert counts[2] == 4 and nz == 128 and nx == 16 and ny % 16 == 0 and ny <= HALF
    points = source_cells.shape[0]
    air = jax.ShapeDtypeStruct((nx, ny, nz), F32)
    plate = jax.ShapeDtypeStruct((nx, ny), F32)
    tall = ny + 2 * PAD
    vmem = pltpu.VMEM
    sheet = vmem((nx, ny), F32)
    block = vmem((nx, ny, nz), F32)
    scratch = [
        block, vmem((2, nx, tall, nz), F32), block, vmem((STEPS, nx, ny, nz), F32), block,
        vmem((nx, tall, nz), F32), block, block, block,
        sheet, sheet, sheet, sheet, sheet, vmem((nx, ny), jnp.int32), vmem((nx, ny), jnp.int32),
        vmem((1, points), jnp.int32), vmem(source_force.shape, F32),
        vmem((4, nz, nz), F32), vmem((tall, nz), F32), vmem((tall, nz), F32),
        vmem((tall, nz), F32), vmem((STEPS, tall, nz), F32), vmem((nz, nz), F32),
        vmem((STEPS, 2, 2 * ny + 16, nz), F32), vmem((STEPS, 2, 2 * ny + 16, nz), F32),
        vmem((STEPS, 2, 2 * nx + 16, nz), F32), vmem((STEPS, 2, 2 * nx + 16, nz), F32),
        vmem((STEPS, 4, 16, nz), F32),
        vmem((STEPS, 2, ny // 2, nz), F32), vmem((STEPS, 2, ny // 2, nz), F32),
        vmem((STEPS, ny // 2, nz), F32),
        pltpu.SemaphoreType.DMA((14,)),
        pltpu.SemaphoreType.DMA((STEPS, len(KEYS))), pltpu.SemaphoreType.DMA((STEPS, len(KEYS))),
    ]
    anywhere = pl.BlockSpec(memory_space=pl.ANY)
    resident = pl.BlockSpec(memory_space=pltpu.VMEM)
    results = pl.pallas_call(
        functools.partial(kernel, counts),
        out_shape=(air, air, plate, plate, plate),
        in_specs=[anywhere] * 14,
        out_specs=(resident,) * 5,
        scratch_shapes=scratch,
        compiler_params=pltpu.CompilerParams(
            collective_id=0, has_side_effects=True, vmem_limit_bytes=63 * 1024 * 1024
        ),
        cost_estimate=pl.CostEstimate(
            flops=40 * 6 * nx * ny * nz, bytes_accessed=28 * nx * ny * nz, transcendentals=0
        ),
    )(
        press_prev, press_now, board_prev, board_now, costate_prev, costate_now, adjoint_prev,
        adjoint_now, speed, stiffness, plate_mask, height, source_cells.reshape(1, points),
        source_force,
    )
    return pl.pallas_call(
        hand_out,
        out_shape=(air, air, plate, plate, plate),
        in_specs=[resident] * 5,
        out_specs=(anywhere,) * 5,
        scratch_shapes=[pltpu.SemaphoreType.DMA((5,))],
        compiler_params=pltpu.CompilerParams(vmem_limit_bytes=62 * 1024 * 1024),
    )(*results)


def hand_out(*refs):
    sources, targets, sem = refs[:5], refs[5:10], refs[10]
    copies = [
        pltpu.make_async_copy(source, target, sem.at[i])
        for i, (source, target) in enumerate(zip(sources, targets))
    ]
    for copy in copies:
        copy.start()
    for copy in copies:
        copy.wait()


def solution(mesh):
    air, plate = P("gx", "gy", "gz"), P("gx", "gy")
    counts = tuple(mesh.shape[a] for a in ("gx", "gy", "gz"))
    return jax.shard_map(
        functools.partial(on_device, counts),
        mesh=mesh,
        in_specs=(air, air, plate, plate, air, air, plate, plate, air, plate, plate, plate, P(), P()),
        out_specs=(air, air, plate, plate, plate),
        check_vma=False,
    )
```
